32 devices in a mesh: row: 8 (over z, core), col: 4 (over y, x).
Axes of the slice: x: 2, y: 2, z: 4, core: 2. Of those that a mesh axis runs over, the one named last changes fastest.
Arguments:
- covariance: float32 [8192, 8192], P('row', 'col'), may hold values from -3 to 5, as said below
- obs_cells: int32 [2, 8192], P(None, ('row', 'col')), may hold values from 0 to 255
- pred_cells: int32 [2, 512], replicated, may hold values from 0 to 255
- targets: float32 [8192, 256], P(('row', 'col')), may hold values from -1.5 to 1.5
- cross_sum: float32 [8192, 512], P(('row', 'col')), may hold values from -1.8 to 1.8
- prior_mean: float32 [512, 256], replicated, may hold values from -6 to 6
Outputs:
- factor_state: float32 [8192, 8192], P('row', 'col')
- reduced_targets: float32 [8192, 256], P(('row', 'col'))
- cross_next: float32 [8192, 512], P(('row', 'col'))
- predicted: float32 [512, 256], replicated
The draws below stay inside these ranges and needn't reach their ends.
Inputs may be any that keep to these rules, and one draw needn't show every extreme that they name: covariance is symmetric and positive definite.
All inputs are finite; a program needn't handle non-finite values.
Results may differ from the reference program's by a relative error of at most 0.00007.
Values sent between devices are 32-bit elements; how exact they have to be, the bound alone decides.
A program may use at most 128 MiB of HBM per device.

```python
import math
import jax
import jax.numpy as jnp
from jax import lax

TILE = 1024
RHS_COLS = 256
POINTS = 512
GRID = 256
RANGE = 16
ORDER = 8192


def draw_covariance(key, part):
    key_g = jax.random.fold_in(key, 11)
    key_d = jax.random.fold_in(key, 12)
    limit = math.sqrt(3.0)
    factors = jax.random.uniform(key_g, (ORDER, TILE), jnp.float32, -limit, limit)
    diagonal = jnp.exp(jax.random.uniform(key_d, (ORDER,), jnp.float32, math.log(0.5), math.log(2.0)))
    product = jnp.dot(factors, factors.T, precision=jax.lax.Precision.HIGHEST) / TILE
    product = 0.5 * (product + product.T)
    places = jnp.arange(ORDER)
    return product.at[places, places].add(diagonal)


def place_ends(values, key, low, largest):
    index_at = [jax.random.randint(jax.random.fold_in(key, axis), (), 0, length) for axis, length in enumerate(values.shape)]
    main_axis = values.shape.index(max(values.shape))
    neighbour = index_at[:main_axis] + [(index_at[main_axis] + 1) % values.shape[main_axis]] + index_at[main_axis + 1:]
    return values.at[tuple(index_at)].set(low).at[tuple(neighbour)].set(largest)


def shard_levels(own_key, extent, split, low, high):
    gain, own = 1.0, jax.random.fold_in(own_key, 6)
    for dim, shards_of in split:
        steps = jnp.exp(jax.random.uniform(jax.random.fold_in(own, dim), (shards_of,), jnp.float32, low / len(split), high / len(split)))
        gain = gain * jnp.repeat(steps, extent[dim] // shards_of).reshape([-1 if axis == dim else 1 for axis in range(len(extent))])
    return gain


def normal_values(rng, extent, deviation, most, shards=(), kind=jnp.bfloat16):
    array = deviation * jax.random.normal(rng, extent, jnp.float32)
    if shards:
        array = array * shard_levels(rng, extent, shards, -0.22, 0.18)
    return jnp.clip(array, -most, most).astype(kind)


def setup_inputs(seed: int = 0) -> dict:
    seeds = jax.random.split(jax.random.key(seed), 7)
    return {
        "covariance": draw_covariance(jax.random.fold_in(seeds[6], 71), 0),
        "obs_cells": place_ends(jax.random.randint(seeds[1], (2, ORDER), 0, GRID), jax.random.fold_in(seeds[1], 1), 0, GRID - 1).astype(jnp.int32),
        "pred_cells": place_ends(jax.random.randint(seeds[2], (2, POINTS), 0, GRID), jax.random.fold_in(seeds[2], 1), 0, GRID - 1).astype(jnp.int32),
        "targets": normal_values(seeds[3], (ORDER, RHS_COLS), 0.25, 1.5, ((0, 32),), jnp.float32),
        "cross_sum": normal_values(seeds[4], (ORDER, POINTS), 0.3, 1.8, ((0, 32),), jnp.float32),
        "prior_mean": normal_values(seeds[5], (POINTS, RHS_COLS), 1.0, 6.0, (), jnp.float32),
    }


root_three = math.sqrt(3.0)

def matern_tile(cells_a, cells_b):
    first = cells_a.astype(jnp.float32)
    second = cells_b.astype(jnp.float32)
    delta_x = first[0][:, None] - second[0][None, :]
    delta_y = first[1][:, None] - second[1][None, :]
    scaled = jnp.sqrt(delta_x * delta_x + delta_y * delta_y) * (root_three / RANGE)
    return (1.0 + scaled) * jnp.exp(-scaled)

def reference(covariance, obs_cells, pred_cells, targets, cross_sum, prior_mean):
    lead_factor = jnp.linalg.cholesky(covariance[:TILE, :TILE])
    panel = lax.linalg.triangular_solve(lead_factor, covariance[:, :TILE], left_side=False, lower=True, transpose_a=True)
    factor_state = covariance - jnp.dot(panel, panel.T, precision=lax.Precision.HIGHEST)
    factor_state = factor_state.at[:, :TILE].set(panel)
    factor_state = factor_state.at[:TILE, TILE:].set(jnp.zeros((TILE, ORDER - TILE), jnp.float32))
    kernel = matern_tile(obs_cells[:, :TILE], pred_cells)
    stacked = jnp.concatenate([targets[:TILE], kernel - cross_sum[:TILE]], axis=1)
    both = lax.linalg.triangular_solve(lead_factor, stacked, left_side=True, lower=True, transpose_a=False)
    solved = both[:, :RHS_COLS]
    lifted = both[:, RHS_COLS:]
    reduced_targets = targets - jnp.dot(panel, solved, precision=lax.Precision.HIGHEST)
    reduced_targets = reduced_targets.at[:TILE].set(solved)
    cross_next = cross_sum + jnp.dot(panel, lifted, precision=lax.Precision.HIGHEST)
    cross_next = cross_next.at[:TILE].set(lifted)
    predicted = prior_mean + jnp.dot(lifted.T, solved, precision=lax.Precision.HIGHEST)
    return (factor_state, reduced_targets, cross_next, predicted)
```

```python
import math

import jax
import jax.numpy as jnp
from jax import lax
from jax.experimental import pallas as pl
from jax.experimental.pallas import tpu as pltpu
from jax.sharding import PartitionSpec as P

RANGE = 16
BLOCK = 128
GROUP = 8


root_three = math.sqrt(3.0)


def invert_block(block):
    size = block.shape[0]
    groups = size // GROUP
    rows = lax.broadcasted_iota(jnp.int32, (GROUP, size), 0)
    columns = lax.broadcasted_iota(jnp.int32, (GROUP, size), 1)
    left = [block[g * GROUP : (g + 1) * GROUP, :] for g in range(groups)]
    right = [jnp.where(columns == rows + g * GROUP, 1.0, 0.0) for g in range(groups)]
    for g in range(groups):
        first = g * GROUP
        more = g + 1 < groups
        wide = (GROUP, size)
        own = [jnp.broadcast_to(left[g][:, first + k : first + k + 1], wide) for k in range(GROUP)]
        if more:
            following = [
                jnp.broadcast_to(left[g + 1][:, first + k : first + k + 1], wide) for k in range(GROUP)
            ]
        for k in range(GROUP):
            root = lax.rsqrt(jnp.broadcast_to(own[k][k : k + 1, :], wide))
            factor = own[k] * root
            row_left = jnp.broadcast_to(left[g][k : k + 1, :], wide) * root
            row_right = jnp.broadcast_to(right[g][k : k + 1, :], wide) * root
            below = rows > k
            here = rows == k

            def step(old, row):
                return jnp.where(below, old - factor * row, jnp.where(here, row, old))

            if more:
                factor_next = following[k] * root
            for m in range(k + 1, GROUP):
                row = jnp.broadcast_to(own[m][k : k + 1, :], wide) * root
                own[m] = jnp.where(below, own[m] - factor * row, own[m])
                if more:
                    following[m] = following[m] - factor_next * row
            left[g] = step(left[g], row_left)
            right[g] = step(right[g], row_right)
            if more:
                left[g + 1] = left[g + 1] - factor_next * row_left
                right[g + 1] = right[g + 1] - factor_next * row_right
        if g + 2 < groups:
            turned = left[g].T
            for i in range(g + 2, groups):
                for k in range(GROUP):
                    factor = jnp.broadcast_to(turned[i * GROUP : (i + 1) * GROUP, k : k + 1], wide)
                    left[i] = left[i] - factor * jnp.broadcast_to(left[g][k : k + 1, :], wide)
                    right[i] = right[i] - factor * jnp.broadcast_to(right[g][k : k + 1, :], wide)
    return jnp.concatenate(right, axis=0)


def invert_kernel(lead_ref, inverse_ref, work):
    size = lead_ref.shape[0]
    count = size // BLOCK
    work[...] = lead_ref[...]
    columns = lax.broadcasted_iota(jnp.int32, (BLOCK, size), 1)

    @pl.loop(0, count)
    def _(j):
        at = pl.ds(pl.multiple_of(j * BLOCK, BLOCK), BLOCK)
        inverse = invert_block(work[at, at])
        pivot = jnp.dot(inverse, work[at, :], precision=lax.Precision.HIGHEST)
        work[at, :] = pivot
        work[at, at] = inverse
        inverse_ref[at, :] = jnp.where(columns < (j + 1) * BLOCK, work[at, :], 0.0)

        @pl.loop(j + 1, count)
        def _(i):
            to = pl.ds(pl.multiple_of(i * BLOCK, BLOCK), BLOCK)
            factor = work[at, to]
            work[to, at] = jnp.zeros((BLOCK, BLOCK), jnp.float32)
            work[to, :] = work[to, :] - lax.dot_general(
                factor, work[at, :], (((0,), (0,)), ((), ())), precision=lax.Precision.HIGHEST
            )


def invert_factor(lead):
    size = lead.shape[0]
    return pl.pallas_call(
        invert_kernel,
        out_shape=jax.ShapeDtypeStruct((size, size), jnp.float32),
        in_specs=[pl.BlockSpec(memory_space=pltpu.VMEM)],
        out_specs=pl.BlockSpec(memory_space=pltpu.VMEM),
        scratch_shapes=[pltpu.VMEM((size, size), jnp.float32)],
        compiler_params=pltpu.CompilerParams(vmem_limit_bytes=40 * 2**20),
    )(lead)


def spread(block, axis, source):
    block = jnp.where(lax.axis_index(axis) == source, block, jnp.zeros_like(block))
    return lax.psum(block, axis)


def matern_tile(first, second):
    delta_x = first[0][:, None] - second[0][None, :]
    delta_y = first[1][:, None] - second[1][None, :]
    scaled = jnp.sqrt(delta_x * delta_x + delta_y * delta_y) * (root_three / RANGE)
    return (1.0 + scaled) * jnp.exp(-scaled)


def dot(first, second, first_axis, second_axis):
    return lax.dot_general(
        first, second, (((first_axis,), (second_axis,)), ((), ())), precision=lax.Precision.HIGH
    )


def body(covariance, obs_cells, pred_cells, targets, cross_sum, prior_mean):
    tile_size = covariance.shape[0]
    slab = targets.shape[0]
    row_index = lax.axis_index("row")
    column_index = lax.axis_index("col")
    cells_float = obs_cells.astype(jnp.float32)
    panel_in = spread(covariance[:, :tile_size], "col", 0)
    diag_in, top_cov, top_targets, top_cross, top_cells = (
        spread(panel_in, "row", 0),
        spread(covariance, "row", 0),
        spread(targets, "row", 0),
        spread(cross_sum, "row", 0),
        spread(cells_float, "row", 0),
    )
    inverse = invert_factor(diag_in)
    panel_rows = dot(panel_in, inverse, 1, 1)
    panel_columns = dot(inverse, top_cov, 1, 0)
    updated = covariance - dot(panel_rows, panel_columns, 1, 0)
    updated = jnp.where(row_index == 0, jnp.zeros_like(updated), updated)
    first_tile = jnp.where(column_index == 0, panel_rows, updated[:, :tile_size])
    factor_state = jnp.concatenate([first_tile, updated[:, tile_size:]], axis=1)
    lead_targets, lead_cross, lead_cells = (
        lax.all_gather(top_targets, "col", axis=0, tiled=True),
        lax.all_gather(top_cross, "col", axis=0, tiled=True),
        lax.all_gather(top_cells, "col", axis=1, tiled=True),
    )
    kernel = matern_tile(lead_cells, pred_cells.astype(jnp.float32))
    stacked = jnp.concatenate([lead_targets, kernel - lead_cross], axis=1)
    both = dot(inverse, stacked, 1, 0)
    width = targets.shape[1]
    solved = both[:, :width]
    lifted = both[:, width:]
    my_rows = lax.dynamic_slice_in_dim(panel_rows, column_index * slab, slab, 0)
    my_solved = lax.dynamic_slice_in_dim(solved, column_index * slab, slab, 0)
    my_lifted = lax.dynamic_slice_in_dim(lifted, column_index * slab, slab, 0)
    reduced_targets = targets - dot(my_rows, solved, 1, 0)
    reduced_targets = jnp.where(row_index == 0, my_solved, reduced_targets)
    cross_next = cross_sum + dot(my_rows, lifted, 1, 0)
    cross_next = jnp.where(row_index == 0, my_lifted, cross_next)
    predicted = prior_mean + dot(lifted, solved, 0, 0)
    return (factor_state, reduced_targets, cross_next, predicted)


def solution(mesh):
    in_specs = (
        P("row", "col"),
        P(None, ("row", "col")),
        P(),
        P(("row", "col"), None),
        P(("row", "col"), None),
        P(),
    )
    out_specs = (P("row", "col"), P(("row", "col"), None), P(("row", "col"), None), P())
    return jax.shard_map(body, mesh=mesh, in_specs=in_specs, out_specs=out_specs, check_vma=False)
```

```python
import functools
import math

import jax
import jax.numpy as jnp
from jax import lax
from jax.experimental import pallas as pl
from jax.experimental.pallas import tpu as pltpu
from jax.sharding import PartitionSpec as P

RANGE = 16
BLOCK = 128
GROUP = 8
HALVES = 2
MESH = pl.DeviceIdType.MESH


root_three = math.sqrt(3.0)


def invert_block(block):
    size = block.shape[0]
    groups = size // GROUP
    wide = (GROUP, size)
    rows = lax.broadcasted_iota(jnp.int32, wide, 0)
    columns = lax.broadcasted_iota(jnp.int32, wide, 1)
    left = [block[g * GROUP : (g + 1) * GROUP, :] for g in range(groups)]
    right = [jnp.where(columns == rows + g * GROUP, 1.0, 0.0) for g in range(groups)]
    below = [rows > k for k in range(GROUP)]
    here = [rows == k for k in range(GROUP)]
    for g in range(groups):
        first = g * GROUP
        more = g + 1 < groups
        own = [jnp.broadcast_to(left[g][:, first + k : first + k + 1], wide) for k in range(GROUP)]
        if more:
            following = [
                jnp.broadcast_to(left[g + 1][:, first + k : first + k + 1], wide) for k in range(GROUP)
            ]
        for k in range(GROUP):
            root = lax.rsqrt(jnp.broadcast_to(own[k][k : k + 1, :], wide))
            factor = jnp.where(below[k], own[k] * root, 0.0)
            row_left = jnp.broadcast_to(left[g][k : k + 1, :], wide) * root
            row_right = jnp.broadcast_to(right[g][k : k + 1, :], wide) * root
            if more:
                factor_next = following[k] * root
            for m in range(k + 1, GROUP):
                row = jnp.broadcast_to(own[m][k : k + 1, :], wide) * root
                own[m] = own[m] - factor * row
                if more:
                    following[m] = following[m] - factor_next * row
            left[g] = jnp.where(here[k], row_left, left[g] - factor * row_left)
            right[g] = jnp.where(here[k], row_right, right[g] - factor * row_right)
            if more:
                left[g + 1] = left[g + 1] - factor_next * row_left
                right[g + 1] = right[g + 1] - factor_next * row_right
        if g + 2 < groups:
            turned = left[g].T[(g + 2) * GROUP :, :]
            rest = groups - g - 2
            tall = (rest * GROUP, size)
            rest_left = jnp.concatenate(left[g + 2 :], axis=0)
            rest_right = jnp.concatenate(right[g + 2 :], axis=0)
            for k in range(GROUP):
                factor = jnp.broadcast_to(turned[:, k : k + 1], tall)
                rest_left = rest_left - factor * left[g][k : k + 1, :]
                rest_right = rest_right - factor * right[g][k : k + 1, :]
            for i in range(rest):
                left[g + 2 + i] = rest_left[i * GROUP : (i + 1) * GROUP, :]
                right[g + 2 + i] = rest_right[i * GROUP : (i + 1) * GROUP, :]
    return jnp.concatenate(right, axis=0)


def invert_step(j, work, inverse_ref):
    size = work.shape[0]
    at = pl.ds(pl.multiple_of(j * BLOCK, BLOCK), BLOCK)
    columns = lax.broadcasted_iota(jnp.int32, (BLOCK, size), 1)
    inverse = invert_block(work[at, at])
    pivot = jnp.dot(inverse, work[at, :], precision=lax.Precision.HIGHEST)
    work[at, :] = pivot
    work[at, at] = inverse
    inverse_ref[at, :] = jnp.where(columns < (j + 1) * BLOCK, work[at, :], 0.0)


def update_step(j, work):
    size = work.shape[0]
    at = pl.ds(pl.multiple_of(j * BLOCK, BLOCK), BLOCK)

    @pl.loop(j + 1, size // BLOCK)
    def _(i):
        to = pl.ds(pl.multiple_of(i * BLOCK, BLOCK), BLOCK)
        factor = work[at, to]
        work[to, at] = jnp.zeros((BLOCK, BLOCK), jnp.float32)
        work[to, :] = work[to, :] - lax.dot_general(
            factor, work[at, :], (((0,), (0,)), ((), ())), precision=lax.Precision.HIGHEST
        )


def pick(index, table):
    found = 0
    for place, value in enumerate(table):
        found = found + jnp.where(index == place, value, 0)
    return found


def exchange_kernel(
    shape, cov, slab, panel, top, rhs, inverse, work, made, local_sem,
    panel_recv, left_recv, right_recv, inv_recv, slab_recv,
    panel_send, left_send, right_send, inv_send, slab_send,
):
    row_count, col_count = shape
    row, col = lax.axis_index("row"), lax.axis_index("col")
    size = panel.shape[0]
    count = size // BLOCK
    slab_rows = slab.shape[0]
    even = lax.rem(row, 2) == 0
    odd = jnp.logical_not(even)
    mate = row + 1 - 2 * lax.rem(row, 2)
    is_lead = jnp.logical_and(row == 0, col == 0)
    both = jnp.logical_and
    has_down = row + 2 < row_count

    barrier = pltpu.get_barrier_semaphore()

    def greet(r, c):
        pl.semaphore_signal(barrier, inc=1, device_id=(r, c), device_id_type=MESH)

    for shift in range(1, col_count):
        greet(row, lax.rem(col + shift, col_count))
    greet(mate, col)
    pl.when(row >= 2)(lambda: greet(row - 2, col))
    pl.when(has_down)(lambda: greet(row + 2, col))
    pl.semaphore_wait(barrier, col_count + jnp.where(row >= 2, 1, 0) + jnp.where(has_down, 1, 0))

    pending = []

    def send(condition, source, target, send_sem, recv_sem, r, c, waited=None):
        def make():
            return pltpu.make_async_remote_copy(
                src_ref=source, dst_ref=target, send_sem=send_sem, recv_sem=recv_sem,
                device_id=(r, c), device_id_type=MESH,
            )

        pl.when(condition)(lambda: make().start())
        if waited is None:
            pending.append((condition, make))
        elif waited is not False:
            pending.append((waited, make))

    def arrive(condition, target, recv_sem):
        def wait():
            pltpu.make_async_copy(target, target, recv_sem).wait()

        pl.when(condition)(wait)

    order = [i ^ (i >> 1) for i in range(col_count)]
    if sorted(order) != list(range(col_count)):
        order = list(range(col_count))
    onward, backward = [0] * col_count, [0] * col_count
    for i in range(col_count):
        onward[order[i]] = order[(i + 1) % col_count]
        backward[order[i]] = order[(i - 1) % col_count]
    next_col = jnp.where(even, pick(col, onward), pick(col, backward))

    def rows_of(t):
        return pl.ds(t * BLOCK, BLOCK)

    lead_cols, right_cols = pl.ds(0, size), pl.ds(size, top.shape[1] - size)

    def send_panel(condition, source, t):
        go = both(condition, next_col != 0)
        at = rows_of(t)
        send(go, source.at[at, lead_cols], panel.at[at], panel_send.at[t], panel_recv.at[t], row, next_col)

    def send_top(row_zero, t):
        at = rows_of(t)
        source = cov if row_zero else top
        here = row == 0 if row_zero else row > 0
        left, right = (at, lead_cols), (at, right_cols)
        go = both(here, even)
        send(both(go, has_down), source.at[left], top.at[left], left_send.at[0, t], left_recv.at[t], row + 2, col)
        send(go, source.at[left], top.at[left], left_send.at[1, t], left_recv.at[t], mate, col)
        if row_zero:
            send(here, source.at[right], top.at[right], right_send.at[0, t], right_recv.at[t], mate, col)
        else:
            go = both(here, odd)
            send(both(go, has_down), source.at[right], top.at[right], right_send.at[1, t], right_recv.at[t], row + 2, col)
            send(both(go, row > 1), source.at[right], top.at[right], right_send.at[2, t], right_recv.at[t], mate, col)

    levels = 0
    while (1 << levels) < col_count:
        levels += 1

    def send_inverse(condition, source, j, half, waits):
        at = (pl.ds(j * BLOCK + half * (BLOCK // HALVES), BLOCK // HALVES), pl.ds(0, (j + 1) * BLOCK))
        number = j * HALVES + half

        def to(where, slot, r, c):
            where = both(even, where)
            send(
                both(condition, where), source.at[at], inverse.at[at], inv_send.at[slot, number],
                inv_recv.at[number], r, c, where if waits else False,
            )

        to(both(col == 0, has_down), 0, row + 2, col)
        for level in range(levels):
            child = col + (1 << level)
            to(both(col < (1 << level), child < col_count), 1 + level, row, child)
        to(even, 1 + levels, mate, col)

    def slab_at(c):
        return rhs.at[pl.ds(pl.multiple_of(c * slab_rows, slab_rows), slab_rows)]

    lead_copy = pltpu.make_async_copy(cov.at[:, lead_cols], work, local_sem.at[0])
    panel_copy = pltpu.make_async_copy(cov.at[:, lead_cols], panel, local_sem.at[1])
    top_copy = pltpu.make_async_copy(cov, top, local_sem.at[2])
    slab_copy = pltpu.make_async_copy(slab, slab_at(col), local_sem.at[3])
    made_copy = pltpu.make_async_copy(made, inverse, local_sem.at[4])

    def send_slab(condition, source):
        own = slab_at(col)
        send(both(condition, has_down), source, own, slab_send.at[0], slab_recv.at[col], row + 2, col)
        for shift in range(1, col_count):
            send(condition, source, own, slab_send.at[shift], slab_recv.at[col], row, lax.rem(col + shift, col_count))
        send(condition, source, own, slab_send.at[col_count], slab_recv.at[col], mate, col)

    pl.when(is_lead)(lambda: lead_copy.start())
    for t in range(count):
        send_panel(col == 0, cov, t)
        send_top(True, t)
        if t == 0:
            send_slab(row == 0, slab)
    pl.when(col == 0)(lambda: panel_copy.start())
    pl.when(row == 0)(lambda: top_copy.start())
    pl.when(row == 0)(lambda: slab_copy.start())

    @pl.when(is_lead)
    def _():
        lead_copy.wait()

        @pl.loop(0, count)
        def _(j):
            invert_step(j, work, made)
            for step in range(count):

                @pl.when(j == step)
                def _():
                    for half in range(HALVES):
                        send_inverse(is_lead, made, step, half, False)

            update_step(j, work)

        made_copy.start()

    follows = jnp.logical_not(is_lead)
    lower = both(even, row > 0)
    for t in range(count):
        arrive(col > 0, panel.at[rows_of(t)], panel_recv.at[t])
        send_panel(col > 0, panel, t)
        for half in range(HALVES):
            at = (pl.ds(t * BLOCK + half * (BLOCK // HALVES), BLOCK // HALVES), pl.ds(0, (t + 1) * BLOCK))
            arrive(follows, inverse.at[at], inv_recv.at[t * HALVES + half])
            send_inverse(follows, inverse, t, half, True)
        arrive(lower, top.at[rows_of(t), lead_cols], left_recv.at[t])
        arrive(odd, top.at[rows_of(t), right_cols], right_recv.at[t])
        send_top(False, t)
        if t == min(1, count - 1):
            arrive(lower, slab_at(col), slab_recv.at[col])
            send_slab(lower, slab_at(col))
    for shift in range(1, col_count):
        other = lax.rem(col + shift, col_count)
        arrive(even, slab_at(other), slab_recv.at[other])
        send(
            even, slab_at(other), slab_at(other), slab_send.at[col_count + shift], slab_recv.at[other], mate, col
        )
    for t in range(count):
        arrive(odd, top.at[rows_of(t), lead_cols], left_recv.at[t])
        arrive(lower, top.at[rows_of(t), right_cols], right_recv.at[t])
    for c in range(col_count):
        arrive(odd, slab_at(c), slab_recv.at[c])
    for condition, make in pending:
        pl.when(condition)(lambda make=make: make().wait_send())
    pl.when(is_lead)(lambda: made_copy.wait())
    pl.when(col == 0)(lambda: panel_copy.wait())
    pl.when(row == 0)(lambda: top_copy.wait())
    pl.when(row == 0)(lambda: slab_copy.wait())


def exchange(shape, covariance, slab):
    size = covariance.shape[0]
    count = size // BLOCK
    slots = shape[1].bit_length() + 2
    f32 = jnp.float32
    dma = pltpu.SemaphoreType.DMA
    anywhere = pl.BlockSpec(memory_space=pl.ANY)
    return pl.pallas_call(
        functools.partial(exchange_kernel, shape),
        out_shape=(
            jax.ShapeDtypeStruct((size, size), f32),
            jax.ShapeDtypeStruct(covariance.shape, f32),
            jax.ShapeDtypeStruct((slab.shape[0] * shape[1], slab.shape[1]), f32),
            jax.ShapeDtypeStruct((size, size), f32),
        ),
        in_specs=[anywhere] * 2,
        out_specs=[anywhere] * 4,
        scratch_shapes=[
            pltpu.VMEM((size, size), f32),
            pltpu.VMEM((size, size), f32),
            dma((5,)),
            dma((count,)),
            dma((count,)),
            dma((count,)),
            dma((count * HALVES,)),
            dma((shape[1],)),
            dma((count,)),
            dma((2, count)),
            dma((3, count)),
            dma((slots, count * HALVES)),
            dma((2 * shape[1],)),
        ],
        compiler_params=pltpu.CompilerParams(
            collective_id=0, has_side_effects=True, vmem_limit_bytes=48 * 2**20
        ),
    )(covariance, slab)


def matern_tile(first, second):
    delta_x = first[0][:, None] - second[0][None, :]
    delta_y = first[1][:, None] - second[1][None, :]
    scaled = jnp.sqrt(delta_x * delta_x + delta_y * delta_y) * (root_three / RANGE)
    return (1.0 + scaled) * jnp.exp(-scaled)


def dot(first, second, first_axis, second_axis):
    return lax.dot_general(
        first, second, (((first_axis,), (second_axis,)), ((), ())), precision=lax.Precision.HIGH
    )


def body(shape, covariance, obs_cells, pred_cells, targets, cross_sum, prior_mean):
    tile_size = covariance.shape[0]
    slab = targets.shape[0]
    row_index = lax.axis_index("row")
    column_index = lax.axis_index("col")
    kernel = matern_tile(obs_cells.astype(jnp.float32), pred_cells.astype(jnp.float32))
    stacked = jnp.concatenate([targets, kernel - cross_sum], axis=1)
    panel_in, top_cov, lead_stacked, inverse = exchange(shape, covariance, stacked)
    inverse = jnp.tril(inverse)
    panel_rows = dot(panel_in, inverse, 1, 1)
    panel_columns = dot(inverse, top_cov, 1, 0)
    updated = covariance - dot(panel_rows, panel_columns, 1, 0)
    updated = jnp.where(row_index == 0, jnp.zeros_like(updated), updated)
    first_tile = jnp.where(column_index == 0, panel_rows, updated[:, :tile_size])
    factor_state = lax.dynamic_update_slice(updated, first_tile, (0, 0))
    both = dot(inverse, lead_stacked, 1, 0)
    width = targets.shape[1]
    solved = both[:, :width]
    lifted = both[:, width:]
    my_rows = lax.dynamic_slice_in_dim(panel_rows, column_index * slab, slab, 0)
    my_solved = lax.dynamic_slice_in_dim(solved, column_index * slab, slab, 0)
    my_lifted = lax.dynamic_slice_in_dim(lifted, column_index * slab, slab, 0)
    reduced_targets = targets - dot(my_rows, solved, 1, 0)
    reduced_targets = jnp.where(row_index == 0, my_solved, reduced_targets)
    cross_next = cross_sum + dot(my_rows, lifted, 1, 0)
    cross_next = jnp.where(row_index == 0, my_lifted, cross_next)
    predicted = prior_mean + dot(lifted, solved, 0, 0)
    return (factor_state, reduced_targets, cross_next, predicted)


def solution(mesh):
    shape = (mesh.shape["row"], mesh.shape["col"])
    in_specs = (
        P("row", "col"),
        P(None, ("row", "col")),
        P(),
        P(("row", "col"), None),
        P(("row", "col"), None),
        P(),
    )
    out_specs = (P("row", "col"), P(("row", "col"), None), P(("row", "col"), None), P())
    return jax.shard_map(
        functools.partial(body, shape), mesh=mesh, in_specs=in_specs, out_specs=out_specs, check_vma=False)
```

```python
import functools
import math

import jax
import jax.numpy as jnp
from jax import lax
from jax.experimental import pallas as pl
from jax.experimental.pallas import tpu as pltpu
from jax.sharding import PartitionSpec as P

RANGE = 16
BLOCK = 128
GROUP = 8
HALVES = 2
MESH = pl.DeviceIdType.MESH


root_three = math.sqrt(3.0)


def invert_block(block):
    size = block.shape[0]
    groups = size // GROUP
    wide = (GROUP, size)
    rows = lax.broadcasted_iota(jnp.int32, wide, 0)
    columns = lax.broadcasted_iota(jnp.int32, wide, 1)
    left = [block[g * GROUP : (g + 1) * GROUP, :] for g in range(groups)]
    right = [jnp.where(columns == rows + g * GROUP, 1.0, 0.0) for g in range(groups)]
    below = [rows > k for k in range(GROUP)]
    here = [rows == k for k in range(GROUP)]
    for g in range(groups):
        first = g * GROUP
        more = g + 1 < groups
        own = [jnp.broadcast_to(left[g][:, first + k : first + k + 1], wide) for k in range(GROUP)]
        if more:
            following = [
                jnp.broadcast_to(left[g + 1][:, first + k : first + k + 1], wide) for k in range(GROUP)
            ]
        for k in range(GROUP):
            root = lax.rsqrt(jnp.broadcast_to(own[k][k : k + 1, :], wide))
            factor = jnp.where(below[k], own[k] * root, 0.0)
            row_left = jnp.broadcast_to(left[g][k : k + 1, :], wide) * root
            row_right = jnp.broadcast_to(right[g][k : k + 1, :], wide) * root
            if more:
                factor_next = following[k] * root
            for m in range(k + 1, GROUP):
                row = jnp.broadcast_to(own[m][k : k + 1, :], wide) * root
                own[m] = own[m] - factor * row
                if more:
                    following[m] = following[m] - factor_next * row
            left[g] = jnp.where(here[k], row_left, left[g] - factor * row_left)
            right[g] = jnp.where(here[k], row_right, right[g] - factor * row_right)
            if more:
                left[g + 1] = left[g + 1] - factor_next * row_left
                right[g + 1] = right[g + 1] - factor_next * row_right
        if g + 2 < groups:
            turned = left[g].T[(g + 2) * GROUP :, :]
            rest = groups - g - 2
            tall = (rest * GROUP, size)
            rest_left = jnp.concatenate(left[g + 2 :], axis=0)
            rest_right = jnp.concatenate(right[g + 2 :], axis=0)
            for k in range(GROUP):
                factor = jnp.broadcast_to(turned[:, k : k + 1], tall)
                rest_left = rest_left - factor * left[g][k : k + 1, :]
                rest_right = rest_right - factor * right[g][k : k + 1, :]
            for i in range(rest):
                left[g + 2 + i] = rest_left[i * GROUP : (i + 1) * GROUP, :]
                right[g + 2 + i] = rest_right[i * GROUP : (i + 1) * GROUP, :]
    return jnp.concatenate(right, axis=0)


def invert_step(j, work, inverse_ref):
    size = work.shape[0]
    at = pl.ds(pl.multiple_of(j * BLOCK, BLOCK), BLOCK)
    columns = lax.broadcasted_iota(jnp.int32, (BLOCK, size), 1)
    inverse = invert_block(work[at, at])
    pivot = jnp.dot(inverse, work[at, :], precision=lax.Precision.HIGHEST)
    work[at, :] = pivot
    work[at, at] = inverse
    inverse_ref[at, :] = jnp.where(columns < (j + 1) * BLOCK, work[at, :], 0.0)


def update_step(j, work):
    size = work.shape[0]
    at = pl.ds(pl.multiple_of(j * BLOCK, BLOCK), BLOCK)

    @pl.loop(j + 1, size // BLOCK)
    def _(i):
        to = pl.ds(pl.multiple_of(i * BLOCK, BLOCK), BLOCK)
        factor = work[at, to]
        work[to, at] = jnp.zeros((BLOCK, BLOCK), jnp.float32)
        work[to, :] = work[to, :] - lax.dot_general(
            factor, work[at, :], (((0,), (0,)), ((), ())), precision=lax.Precision.HIGHEST
        )


def pick(index, table):
    found = 0
    for place, value in enumerate(table):
        found = found + jnp.where(index == place, value, 0)
    return found


def exchange_kernel(
    shape, cov, slab, panel, top, rhs, inverse, work, local_sem,
    panel_recv, left_recv, right_recv, inv_recv, slab_recv,
    panel_send, left_send, right_send, inv_send, slab_send,
):
    row_count, col_count = shape
    row, col = lax.axis_index("row"), lax.axis_index("col")
    size = panel.shape[0]
    count = size // BLOCK
    slab_rows = slab.shape[0]
    even = lax.rem(row, 2) == 0
    odd = jnp.logical_not(even)
    mate = row + 1 - 2 * lax.rem(row, 2)
    is_lead = jnp.logical_and(row == 0, col == 0)
    both = jnp.logical_and
    has_down = row + 2 < row_count

    barrier = pltpu.get_barrier_semaphore()

    def greet(r, c):
        pl.semaphore_signal(barrier, inc=1, device_id=(r, c), device_id_type=MESH)

    for shift in range(1, col_count):
        greet(row, lax.rem(col + shift, col_count))
    greet(mate, col)
    pl.when(row >= 2)(lambda: greet(row - 2, col))
    pl.when(has_down)(lambda: greet(row + 2, col))
    pl.semaphore_wait(barrier, col_count + jnp.where(row >= 2, 1, 0) + jnp.where(has_down, 1, 0))

    pending = []

    def send(condition, source, target, send_sem, recv_sem, r, c, waited=None):
        def make():
            return pltpu.make_async_remote_copy(
                src_ref=source, dst_ref=target, send_sem=send_sem, recv_sem=recv_sem,
                device_id=(r, c), device_id_type=MESH,
            )

        pl.when(condition)(lambda: make().start())
        if waited is None:
            pending.append((condition, make))
        elif waited is not False:
            pending.append((waited, make))

    def arrive(condition, target, recv_sem):
        def wait():
            pltpu.make_async_copy(target, target, recv_sem).wait()

        pl.when(condition)(wait)

    order = [i ^ (i >> 1) for i in range(col_count)]
    if sorted(order) != list(range(col_count)):
        order = list(range(col_count))
    onward, backward = [0] * col_count, [0] * col_count
    for i in range(col_count):
        onward[order[i]] = order[(i + 1) % col_count]
        backward[order[i]] = order[(i - 1) % col_count]
    next_col = jnp.where(even, pick(col, onward), pick(col, backward))

    def rows_of(t):
        return pl.ds(t * BLOCK, BLOCK)

    lead_cols, right_cols = pl.ds(0, size), pl.ds(size, top.shape[1] - size)

    def send_panel(condition, t):
        go = both(condition, next_col != 0)
        at = rows_of(t)
        send(go, panel.at[at], panel.at[at], panel_send.at[t], panel_recv.at[t], row, next_col)

    def send_top(row_zero, t):
        at = rows_of(t)
        here = row == 0 if row_zero else row > 0
        left, right = (at, lead_cols), (at, right_cols)
        go = both(here, even)
        send(both(go, has_down), top.at[left], top.at[left], left_send.at[0, t], left_recv.at[t], row + 2, col)
        send(go, top.at[left], top.at[left], left_send.at[1, t], left_recv.at[t], mate, col)
        if row_zero:
            send(here, top.at[right], top.at[right], right_send.at[0, t], right_recv.at[t], mate, col)
        else:
            go = both(here, odd)
            send(both(go, has_down), top.at[right], top.at[right], right_send.at[1, t], right_recv.at[t], row + 2, col)
            send(both(go, row > 1), top.at[right], top.at[right], right_send.at[2, t], right_recv.at[t], mate, col)

    levels = 0
    while (1 << levels) < col_count:
        levels += 1

    def send_inverse(condition, j, half, waits):
        at = (pl.ds(j * BLOCK + half * (BLOCK // HALVES), BLOCK // HALVES), pl.ds(0, (j + 1) * BLOCK))
        number = j * HALVES + half

        def to(where, slot, r, c):
            where = both(even, where)
            send(
                both(condition, where), inverse.at[at], inverse.at[at], inv_send.at[slot, number],
                inv_recv.at[number], r, c, where if waits else False,
            )

        to(both(col == 0, has_down), 0, row + 2, col)
        for level in range(levels):
            child = col + (1 << level)
            to(both(col < (1 << level), child < col_count), 1 + level, row, child)
        to(even, 1 + levels, mate, col)

    def slab_at(c):
        return rhs.at[pl.ds(pl.multiple_of(c * slab_rows, slab_rows), slab_rows)]

    lead_copy = pltpu.make_async_copy(cov.at[:, lead_cols], work, local_sem.at[0])
    panel_copy = pltpu.make_async_copy(cov.at[:, lead_cols], panel, local_sem.at[1])
    top_copy = pltpu.make_async_copy(cov, top, local_sem.at[2])
    slab_copy = pltpu.make_async_copy(slab, slab_at(col), local_sem.at[3])

    def send_slab(condition):
        source = slab_at(col)
        own = slab_at(col)
        send(both(condition, has_down), source, own, slab_send.at[0], slab_recv.at[col], row + 2, col)
        for shift in range(1, col_count):
            send(condition, source, own, slab_send.at[shift], slab_recv.at[col], row, lax.rem(col + shift, col_count))
        send(condition, source, own, slab_send.at[col_count], slab_recv.at[col], mate, col)

    pl.when(is_lead)(lambda: lead_copy.start())
    pl.when(col == 0)(lambda: panel_copy.start())
    pl.when(row == 0)(lambda: top_copy.start())
    pl.when(row == 0)(lambda: slab_copy.start())
    pl.when(col == 0)(lambda: panel_copy.wait())
    pl.when(row == 0)(lambda: top_copy.wait())
    pl.when(row == 0)(lambda: slab_copy.wait())
    for t in range(count):
        send_panel(col == 0, t)
        send_top(True, t)
        if t == 0:
            send_slab(row == 0)

    @pl.when(is_lead)
    def _():
        lead_copy.wait()

        @pl.loop(0, count)
        def _(j):
            invert_step(j, work, inverse)
            for step in range(count):

                @pl.when(j == step)
                def _():
                    for half in range(HALVES):
                        send_inverse(is_lead, step, half, False)

            update_step(j, work)

    follows = jnp.logical_not(is_lead)
    lower = both(even, row > 0)
    for t in range(count):
        arrive(col > 0, panel.at[rows_of(t)], panel_recv.at[t])
        send_panel(col > 0, t)
        for half in range(HALVES):
            at = (pl.ds(t * BLOCK + half * (BLOCK // HALVES), BLOCK // HALVES), pl.ds(0, (t + 1) * BLOCK))
            arrive(follows, inverse.at[at], inv_recv.at[t * HALVES + half])
            send_inverse(follows, t, half, True)
        arrive(lower, top.at[rows_of(t), lead_cols], left_recv.at[t])
        arrive(odd, top.at[rows_of(t), right_cols], right_recv.at[t])
        send_top(False, t)
        if t == min(1, count - 1):
            arrive(lower, slab_at(col), slab_recv.at[col])
            send_slab(lower)
    for shift in range(1, col_count):
        other = lax.rem(col + shift, col_count)
        arrive(even, slab_at(other), slab_recv.at[other])
        send(
            even, slab_at(other), slab_at(other), slab_send.at[col_count + shift], slab_recv.at[other], mate, col
        )
    for t in range(count):
        arrive(odd, top.at[rows_of(t), lead_cols], left_recv.at[t])
        arrive(lower, top.at[rows_of(t), right_cols], right_recv.at[t])
    for c in range(col_count):
        arrive(odd, slab_at(c), slab_recv.at[c])
    for condition, make in pending:
        pl.when(condition)(lambda make=make: make().wait_send())


def exchange(shape, covariance, slab):
    size = covariance.shape[0]
    count = size // BLOCK
    slots = shape[1].bit_length() + 2
    f32 = jnp.float32
    dma = pltpu.SemaphoreType.DMA
    anywhere = pl.BlockSpec(memory_space=pl.ANY)
    return pl.pallas_call(
        functools.partial(exchange_kernel, shape),
        out_shape=(
            jax.ShapeDtypeStruct((size, size), f32),
            jax.ShapeDtypeStruct(covariance.shape, f32),
            jax.ShapeDtypeStruct((slab.shape[0] * shape[1], slab.shape[1]), f32),
            jax.ShapeDtypeStruct((size, size), f32),
        ),
        in_specs=[anywhere] * 2,
        out_specs=[pl.BlockSpec(memory_space=pltpu.VMEM)] * 4,
        scratch_shapes=[
            pltpu.VMEM((size, size), f32),
            dma((4,)),
            dma((count,)),
            dma((count,)),
            dma((count,)),
            dma((count * HALVES,)),
            dma((shape[1],)),
            dma((count,)),
            dma((2, count)),
            dma((3, count)),
            dma((slots, count * HALVES)),
            dma((2 * shape[1],)),
        ],
        compiler_params=pltpu.CompilerParams(
            collective_id=0, has_side_effects=True, vmem_limit_bytes=48 * 2**20
        ),
    )(covariance, slab)


def matern_tile(first, second):
    delta_x = first[0][:, None] - second[0][None, :]
    delta_y = first[1][:, None] - second[1][None, :]
    scaled = jnp.sqrt(delta_x * delta_x + delta_y * delta_y) * (root_three / RANGE)
    return (1.0 + scaled) * jnp.exp(-scaled)


def dot(first, second, first_axis, second_axis):
    return lax.dot_general(
        first, second, (((first_axis,), (second_axis,)), ((), ())), precision=lax.Precision.HIGH
    )


def body(shape, covariance, obs_cells, pred_cells, targets, cross_sum, prior_mean):
    tile_size = covariance.shape[0]
    slab = targets.shape[0]
    row_index = lax.axis_index("row")
    column_index = lax.axis_index("col")
    kernel = matern_tile(obs_cells.astype(jnp.float32), pred_cells.astype(jnp.float32))
    stacked = jnp.concatenate([targets, kernel - cross_sum], axis=1)
    panel_in, top_cov, lead_stacked, inverse = exchange(shape, covariance, stacked)
    inverse = jnp.tril(inverse)
    panel_rows = dot(panel_in, inverse, 1, 1)
    panel_columns = dot(inverse, top_cov, 1, 0)
    updated = covariance - dot(panel_rows, panel_columns, 1, 0)
    updated = jnp.where(row_index == 0, jnp.zeros_like(updated), updated)
    first_tile = jnp.where(column_index == 0, panel_rows, updated[:, :tile_size])
    factor_state = lax.dynamic_update_slice(updated, first_tile, (0, 0))
    both = dot(inverse, lead_stacked, 1, 0)
    width = targets.shape[1]
    solved = both[:, :width]
    lifted = both[:, width:]
    my_rows = lax.dynamic_slice_in_dim(panel_rows, column_index * slab, slab, 0)
    my_solved = lax.dynamic_slice_in_dim(solved, column_index * slab, slab, 0)
    my_lifted = lax.dynamic_slice_in_dim(lifted, column_index * slab, slab, 0)
    reduced_targets = targets - dot(my_rows, solved, 1, 0)
    reduced_targets = jnp.where(row_index == 0, my_solved, reduced_targets)
    cross_next = cross_sum + dot(my_rows, lifted, 1, 0)
    cross_next = jnp.where(row_index == 0, my_lifted, cross_next)
    predicted = prior_mean + dot(lifted, solved, 0, 0)
    return (factor_state, reduced_targets, cross_next, predicted)


def solution(mesh):
    shape = (mesh.shape["row"], mesh.shape["col"])
    in_specs = (
        P("row", "col"),
        P(None, ("row", "col")),
        P(),
        P(("row", "col"), None),
        P(("row", "col"), None),
        P(),
    )
    out_specs = (P("row", "col"), P(("row", "col"), None), P(("row", "col"), None), P())
    return jax.shard_map(
        functools.partial(body, shape), mesh=mesh, in_specs=in_specs, out_specs=out_specs, check_vma=False)
```

```python
import functools
import math

import jax
import jax.numpy as jnp
from jax import lax
from jax.experimental import pallas as pl
from jax.experimental.pallas import tpu as pltpu
from jax.sharding import PartitionSpec as P

RANGE = 16
BLOCK = 128
GROUP = 8
HALVES = 2
MESH = pl.DeviceIdType.MESH


root_three = math.sqrt(3.0)


def invert_block(block):
    size = block.shape[0]
    groups = size // GROUP
    wide = (GROUP, size)
    rows = lax.broadcasted_iota(jnp.int32, wide, 0)
    columns = lax.broadcasted_iota(jnp.int32, wide, 1)
    left = [block[g * GROUP : (g + 1) * GROUP, :] for g in range(groups)]
    right = [jnp.where(columns == rows + g * GROUP, 1.0, 0.0) for g in range(groups)]
    below = [rows > k for k in range(GROUP)]
    here = [rows == k for k in range(GROUP)]
    for g in range(groups):
        first = g * GROUP
        more = g + 1 < groups
        own = [jnp.broadcast_to(left[g][:, first + k : first + k + 1], wide) for k in range(GROUP)]
        if more:
            following = [
                jnp.broadcast_to(left[g + 1][:, first + k : first + k + 1], wide) for k in range(GROUP)
            ]
        for k in range(GROUP):
            root = lax.rsqrt(jnp.broadcast_to(own[k][k : k + 1, :], wide))
            factor = jnp.where(below[k], own[k] * root, 0.0)
            row_left = jnp.broadcast_to(left[g][k : k + 1, :], wide) * root
            row_right = jnp.broadcast_to(right[g][k : k + 1, :], wide) * root
            if more:
                factor_next = following[k] * root
            for m in range(k + 1, GROUP):
                row = jnp.broadcast_to(own[m][k : k + 1, :], wide) * root
                own[m] = own[m] - factor * row
                if more:
                    following[m] = following[m] - factor_next * row
            left[g] = jnp.where(here[k], row_left, left[g] - factor * row_left)
            right[g] = jnp.where(here[k], row_right, right[g] - factor * row_right)
            if more:
                left[g + 1] = left[g + 1] - factor_next * row_left
                right[g + 1] = right[g + 1] - factor_next * row_right
        if g + 2 < groups:
            turned = left[g].T[(g + 2) * GROUP :, :]
            rest = groups - g - 2
            tall = (rest * GROUP, size)
            rest_left = jnp.concatenate(left[g + 2 :], axis=0)
            rest_right = jnp.concatenate(right[g + 2 :], axis=0)
            for k in range(GROUP):
                factor = jnp.broadcast_to(turned[:, k : k + 1], tall)
                rest_left = rest_left - factor * left[g][k : k + 1, :]
                rest_right = rest_right - factor * right[g][k : k + 1, :]
            for i in range(rest):
                left[g + 2 + i] = rest_left[i * GROUP : (i + 1) * GROUP, :]
                right[g + 2 + i] = rest_right[i * GROUP : (i + 1) * GROUP, :]
    return jnp.concatenate(right, axis=0)


def invert_step(j, work, inverse_ref):
    size = work.shape[0]
    at = pl.ds(pl.multiple_of(j * BLOCK, BLOCK), BLOCK)
    columns = lax.broadcasted_iota(jnp.int32, (BLOCK, size), 1)
    inverse = invert_block(work[at, at])
    pivot = jnp.dot(inverse, work[at, :], precision=lax.Precision.HIGHEST)
    work[at, :] = pivot
    work[at, at] = inverse
    inverse_ref[at, :] = jnp.where(columns < (j + 1) * BLOCK, work[at, :], 0.0)


def update_step(j, work):
    size = work.shape[0]
    at = pl.ds(pl.multiple_of(j * BLOCK, BLOCK), BLOCK)

    @pl.loop(j + 1, size // BLOCK)
    def _(i):
        to = pl.ds(pl.multiple_of(i * BLOCK, BLOCK), BLOCK)
        factor = work[at, to]
        work[to, at] = jnp.zeros((BLOCK, BLOCK), jnp.float32)
        work[to, :] = work[to, :] - lax.dot_general(
            factor, work[at, :], (((0,), (0,)), ((), ())), precision=lax.Precision.HIGHEST
        )


def pick(index, table):
    found = 0
    for place, value in enumerate(table):
        found = found + jnp.where(index == place, value, 0)
    return found


def exchange_kernel(
    shape, cov, slab, panel, top, rhs, inverse, work, local_sem,
    panel_recv, left_recv, right_recv, inv_recv, slab_recv,
    panel_send, left_send, right_send, inv_send, slab_send,
):
    row_count, col_count = shape
    row, col = lax.axis_index("row"), lax.axis_index("col")
    size = panel.shape[0]
    count = size // BLOCK
    slab_rows = slab.shape[0]
    even = lax.rem(row, 2) == 0
    odd = jnp.logical_not(even)
    mate = row + 1 - 2 * lax.rem(row, 2)
    is_lead = jnp.logical_and(row == 0, col == 0)
    both = jnp.logical_and
    has_down = row + 2 < row_count

    barrier = pltpu.get_barrier_semaphore()

    def greet(r, c):
        pl.semaphore_signal(barrier, inc=1, device_id=(r, c), device_id_type=MESH)

    for shift in range(1, col_count):
        greet(row, lax.rem(col + shift, col_count))
    greet(mate, col)
    pl.when(row >= 2)(lambda: greet(row - 2, col))
    pl.when(has_down)(lambda: greet(row + 2, col))
    pl.semaphore_wait(barrier, col_count + jnp.where(row >= 2, 1, 0) + jnp.where(has_down, 1, 0))

    pending = []

    def send(condition, source, target, send_sem, recv_sem, r, c, waited=None):
        def make():
            return pltpu.make_async_remote_copy(
                src_ref=source, dst_ref=target, send_sem=send_sem, recv_sem=recv_sem,
                device_id=(r, c), device_id_type=MESH,
            )

        pl.when(condition)(lambda: make().start())
        if waited is None:
            pending.append((condition, make))
        elif waited is not False:
            pending.append((waited, make))

    def gated(gate, waits):
        def start(condition, *rest):
            send(both(gate, condition), *rest, waited=condition if waits else False)

        return start

    def arrive(condition, target, recv_sem):
        def wait():
            pltpu.make_async_copy(target, target, recv_sem).wait()

        pl.when(condition)(wait)

    order = [i ^ (i >> 1) for i in range(col_count)]
    if sorted(order) != list(range(col_count)):
        order = list(range(col_count))
    onward, backward = [0] * col_count, [0] * col_count
    for i in range(col_count):
        onward[order[i]] = order[(i + 1) % col_count]
        backward[order[i]] = order[(i - 1) % col_count]
    next_col = jnp.where(even, pick(col, onward), pick(col, backward))

    def rows_of(t):
        return pl.ds(t * BLOCK, BLOCK)

    lead_cols, right_cols = pl.ds(0, size), pl.ds(size, top.shape[1] - size)

    def send_panel(condition, t, send=send):
        go = both(condition, next_col != 0)
        at = rows_of(t)
        send(go, panel.at[at], panel.at[at], panel_send.at[t], panel_recv.at[t], row, next_col)

    def send_top(row_zero, t, send=send):
        at = rows_of(t)
        here = row == 0 if row_zero else row > 0
        left, right = (at, lead_cols), (at, right_cols)
        go = both(here, even)
        send(both(go, has_down), top.at[left], top.at[left], left_send.at[0, t], left_recv.at[t], row + 2, col)
        send(go, top.at[left], top.at[left], left_send.at[1, t], left_recv.at[t], mate, col)
        if row_zero:
            send(here, top.at[right], top.at[right], right_send.at[0, t], right_recv.at[t], mate, col)
        else:
            go = both(here, odd)
            send(both(go, has_down), top.at[right], top.at[right], right_send.at[1, t], right_recv.at[t], row + 2, col)
            send(both(go, row > 1), top.at[right], top.at[right], right_send.at[2, t], right_recv.at[t], mate, col)

    levels = 0
    while (1 << levels) < col_count:
        levels += 1

    def send_inverse(condition, j, half, waits):
        at = (pl.ds(j * BLOCK + half * (BLOCK // HALVES), BLOCK // HALVES), pl.ds(0, (j + 1) * BLOCK))
        number = j * HALVES + half

        def to(where, slot, r, c):
            where = both(even, where)
            send(
                both(condition, where), inverse.at[at], inverse.at[at], inv_send.at[slot, number],
                inv_recv.at[number], r, c, where if waits else False,
            )

        to(both(col == 0, has_down), 0, row + 2, col)
        for level in range(levels):
            child = col + (1 << level)
            to(both(col < (1 << level), child < col_count), 1 + level, row, child)
        to(even, 1 + levels, mate, col)

    def slab_at(c):
        return rhs.at[pl.ds(pl.multiple_of(c * slab_rows, slab_rows), slab_rows)]

    lead_copy = pltpu.make_async_copy(cov.at[:, lead_cols], work, local_sem.at[0])
    panel_copy = pltpu.make_async_copy(cov.at[:, lead_cols], panel, local_sem.at[1])
    top_copy = pltpu.make_async_copy(cov, top, local_sem.at[2])
    slab_copy = pltpu.make_async_copy(slab, slab_at(col), local_sem.at[3])

    def send_slab(condition):
        source = slab_at(col)
        own = slab_at(col)
        send(both(condition, has_down), source, own, slab_send.at[0], slab_recv.at[col], row + 2, col)
        for shift in range(1, col_count):
            send(condition, source, own, slab_send.at[shift], slab_recv.at[col], row, lax.rem(col + shift, col_count))
        send(condition, source, own, slab_send.at[col_count], slab_recv.at[col], mate, col)

    pl.when(is_lead)(lambda: lead_copy.start())
    pl.when(col == 0)(lambda: panel_copy.start())
    pl.when(row == 0)(lambda: top_copy.start())
    pl.when(row == 0)(lambda: slab_copy.start())
    pl.when(col == 0)(lambda: panel_copy.wait())
    pl.when(row == 0)(lambda: top_copy.wait())
    pl.when(row == 0)(lambda: slab_copy.wait())
    send_panel(col == 0, 0)
    send_top(True, 0)
    send_slab(row == 0)

    def send_sources(gate, t, waits):
        if t < count:
            send_panel(col == 0, t, gated(gate, waits))
            send_top(True, t, gated(gate, waits))

    @pl.when(is_lead)
    def _():
        lead_copy.wait()

        @pl.loop(0, count)
        def _(j):
            invert_step(j, work, inverse)
            for step in range(count):

                @pl.when(j == step)
                def _():
                    for half in range(HALVES):
                        send_inverse(is_lead, step, half, False)
                    send_sources(is_lead, step + 1, False)

            update_step(j, work)

    follows = jnp.logical_not(is_lead)
    lower = both(even, row > 0)
    for t in range(count):
        arrive(col > 0, panel.at[rows_of(t)], panel_recv.at[t])
        send_panel(col > 0, t)
        for half in range(HALVES):
            at = (pl.ds(t * BLOCK + half * (BLOCK // HALVES), BLOCK // HALVES), pl.ds(0, (t + 1) * BLOCK))
            arrive(follows, inverse.at[at], inv_recv.at[t * HALVES + half])
            send_inverse(follows, t, half, True)
        send_sources(follows, t + 1, True)
        arrive(lower, top.at[rows_of(t), lead_cols], left_recv.at[t])
        arrive(odd, top.at[rows_of(t), right_cols], right_recv.at[t])
        send_top(False, t)
        if t == min(3, count - 1):
            arrive(lower, slab_at(col), slab_recv.at[col])
            send_slab(lower)
    for shift in range(1, col_count):
        other = lax.rem(col + shift, col_count)
        arrive(even, slab_at(other), slab_recv.at[other])
        send(
            even, slab_at(other), slab_at(other), slab_send.at[col_count + shift], slab_recv.at[other], mate, col
        )
    for t in range(count):
        arrive(odd, top.at[rows_of(t), lead_cols], left_recv.at[t])
        arrive(lower, top.at[rows_of(t), right_cols], right_recv.at[t])
    for c in range(col_count):
        arrive(odd, slab_at(c), slab_recv.at[c])
    for condition, make in pending:
        pl.when(condition)(lambda make=make: make().wait_send())


def exchange(shape, covariance, slab):
    size = covariance.shape[0]
    count = size // BLOCK
    slots = shape[1].bit_length() + 2
    f32 = jnp.float32
    dma = pltpu.SemaphoreType.DMA
    anywhere = pl.BlockSpec(memory_space=pl.ANY)
    return pl.pallas_call(
        functools.partial(exchange_kernel, shape),
        out_shape=(
            jax.ShapeDtypeStruct((size, size), f32),
            jax.ShapeDtypeStruct(covariance.shape, f32),
            jax.ShapeDtypeStruct((slab.shape[0] * shape[1], slab.shape[1]), f32),
            jax.ShapeDtypeStruct((size, size), f32),
        ),
        in_specs=[anywhere] * 2,
        out_specs=[pl.BlockSpec(memory_space=pltpu.VMEM)] * 4,
        scratch_shapes=[
            pltpu.VMEM((size, size), f32),
            dma((4,)),
            dma((count,)),
            dma((count,)),
            dma((count,)),
            dma((count * HALVES,)),
            dma((shape[1],)),
            dma((count,)),
            dma((2, count)),
            dma((3, count)),
            dma((slots, count * HALVES)),
            dma((2 * shape[1],)),
        ],
        compiler_params=pltpu.CompilerParams(
            collective_id=0, has_side_effects=True, vmem_limit_bytes=48 * 2**20
        ),
    )(covariance, slab)


def matern_tile(first, second):
    delta_x = first[0][:, None] - second[0][None, :]
    delta_y = first[1][:, None] - second[1][None, :]
    scaled = jnp.sqrt(delta_x * delta_x + delta_y * delta_y) * (root_three / RANGE)
    return (1.0 + scaled) * jnp.exp(-scaled)


def dot(first, second, first_axis, second_axis):
    return lax.dot_general(
        first, second, (((first_axis,), (second_axis,)), ((), ())), precision=lax.Precision.HIGH
    )


def body(shape, covariance, obs_cells, pred_cells, targets, cross_sum, prior_mean):
    tile_size = covariance.shape[0]
    slab = targets.shape[0]
    row_index = lax.axis_index("row")
    column_index = lax.axis_index("col")
    kernel = matern_tile(obs_cells.astype(jnp.float32), pred_cells.astype(jnp.float32))
    stacked = jnp.concatenate([targets, kernel - cross_sum], axis=1)
    panel_in, top_cov, lead_stacked, inverse = exchange(shape, covariance, stacked)
    inverse = jnp.tril(inverse)
    panel_rows = dot(panel_in, inverse, 1, 1)
    panel_columns = dot(inverse, top_cov, 1, 0)
    updated = covariance - dot(panel_rows, panel_columns, 1, 0)
    updated = jnp.where(row_index == 0, jnp.zeros_like(updated), updated)
    first_tile = jnp.where(column_index == 0, panel_rows, updated[:, :tile_size])
    factor_state = lax.dynamic_update_slice(updated, first_tile, (0, 0))
    both = dot(inverse, lead_stacked, 1, 0)
    width = targets.shape[1]
    solved = both[:, :width]
    lifted = both[:, width:]
    my_rows = lax.dynamic_slice_in_dim(panel_rows, column_index * slab, slab, 0)
    my_solved = lax.dynamic_slice_in_dim(solved, column_index * slab, slab, 0)
    my_lifted = lax.dynamic_slice_in_dim(lifted, column_index * slab, slab, 0)
    reduced_targets = targets - dot(my_rows, solved, 1, 0)
    reduced_targets = jnp.where(row_index == 0, my_solved, reduced_targets)
    cross_next = cross_sum + dot(my_rows, lifted, 1, 0)
    cross_next = jnp.where(row_index == 0, my_lifted, cross_next)
    predicted = prior_mean + dot(lifted, solved, 0, 0)
    return (factor_state, reduced_targets, cross_next, predicted)


def solution(mesh):
    shape = (mesh.shape["row"], mesh.shape["col"])
    in_specs = (
        P("row", "col"),
        P(None, ("row", "col")),
        P(),
        P(("row", "col"), None),
        P(("row", "col"), None),
        P(),
    )
    out_specs = (P("row", "col"), P(("row", "col"), None), P(("row", "col"), None), P())
    return jax.shard_map(
        functools.partial(body, shape), mesh=mesh, in_specs=in_specs, out_specs=out_specs, check_vma=False)
```
